512 devices in a mesh: dp: 64 (over y, z), tensor: 8 (over x, core).
Axes of the slice: x: 4, y: 4, z: 16, core: 2. Of those that a mesh axis runs over, the one named last changes fastest.
Arguments:
- features: bfloat16 [36864, 8192], P('dp', 'tensor'), may hold values from -6 to 6
- out_grads: bfloat16 [36864, 11264], P('dp', 'tensor'), may hold values from -0.032958984 to 0.032958984
- bases: bfloat16 [8192, 512], P('tensor'), may hold values from -0.0625 to 0.0625
- moment_one: float32 [512, 11264], P('dp', 'tensor'), may hold values from -0.12 to 0.12
- moment_two: float32 [512, 11264], P('dp', 'tensor'), may hold values from 1e-05 to 0.001
Outputs:
- weight_update: bfloat16 [8192, 11264], P('dp', 'tensor')
- new_moment_one: float32 [512, 11264], P('dp', 'tensor')
- new_moment_two: float32 [512, 11264], P('dp', 'tensor')
The draws below stay inside these ranges and needn't reach their ends.
All inputs are finite; a program needn't handle non-finite values.
Results may differ from the reference program's by a relative error of at most 0.0076.
Values may be sent and summed in bfloat16 or wider, within the bound.
No kernel may reach another device: no remote copies, remote signals or barrier semaphores. Data moves between devices by JAX's collectives and lax.ppermute only.
A program may use at most 64 MiB of HBM per device.

```python
import math
import jax
import jax.numpy as jnp

D = 8192
FF = 11264
RANK = 512
STEP = 100
TOKENS = 36864


def level_of(key, dims, shards, smallest, high):
    level = 1.0
    for axis_at, blocks in shards:
        draws = jax.random.uniform(jax.random.fold_in(jax.random.fold_in(key, 6), axis_at), (blocks,), jnp.float32, smallest / len(shards), high / len(shards))
        level = level * jnp.repeat(jnp.exp(draws), dims[axis_at] // blocks).reshape((-1,) + (1,) * (len(dims) - 1 - axis_at))
    return level


def centred(key, shape, spread, bound, pieces=(), held_as=jnp.bfloat16):
    result = spread * jax.random.normal(key, shape, jnp.float32)
    if pieces:
        result = result * level_of(key, shape, pieces, -0.22, 0.18)
    return jnp.clip(result, -bound, bound).astype(held_as)


def setup_inputs(seed: int = 0) -> dict:
    key_of = jax.random.split(jax.random.key(seed), 6)
    features = centred(key_of[0], (TOKENS, D), 1.0, 6.0, ((0, 64), (1, 8)))
    out_grads = centred(key_of[1], (TOKENS, FF), 0.0055, 0.032958984, ((0, 64), (1, 8)))
    bases = centred(key_of[2], (D, RANK), D ** -0.5, 0.0625, ((0, 8),))
    moment_one = centred(key_of[3], (RANK, FF), 0.02, 0.12, ((0, 64), (1, 8)), jnp.float32)
    moment_two = jnp.clip(jnp.exp(math.log(0.001) - 4.6051703 * jax.random.uniform(key_of[4], (RANK, FF), jnp.float32) ** level_of(key_of[4], (RANK, FF), ((0, 64), (1, 8)), -0.2, 0.2)), 9.999999747378752e-06, 0.001)
    return dict(features=features, out_grads=out_grads, bases=bases, moment_one=moment_one, moment_two=moment_two)


def reference(features, out_grads, bases, moment_one, moment_two):
    projected = jnp.dot(features, bases, preferred_element_type=jnp.float32)
    projected_low = projected.astype(jnp.bfloat16)
    reduced = jnp.dot(projected_low.T, out_grads, preferred_element_type=jnp.float32)
    new_moment_one = 0.9 * moment_one + 0.1 * reduced
    new_moment_two = 0.999 * moment_two + 0.001 * reduced * reduced
    first_fix = 1.0 - 0.9 ** STEP
    second_fix = 1.0 - 0.999 ** STEP
    direction = (new_moment_one / first_fix / (jnp.sqrt(new_moment_two / second_fix) + 1e-08)).astype(jnp.bfloat16)
    weight_update = jnp.dot(bases, direction, preferred_element_type=jnp.float32).astype(jnp.bfloat16)
    return (weight_update, new_moment_one, new_moment_two)
```

```python
import jax
import jax.numpy as jnp
from jax import lax
from jax.sharding import Mesh, PartitionSpec as P

STEP = 100
Y, ZH, ZL, X, C = 4, 8, 2, 4, 2
BF16 = jnp.bfloat16
F32 = jnp.float32
AXES = ("y", "zh", "zl", "x", "core")
DP = ("y", "zh", "zl")
TENSOR = ("x", "core")


def exchange(blocks, axes):
    return lax.all_to_all(blocks, axes, 0, 0)


def sum_blocks(blocks):
    return jnp.sum(blocks.astype(F32), axis=0)


def project(features, bases):
    half = features.shape[0] // C
    core = lax.axis_index("core")
    halves = features.reshape(X, C, half // X, -1)
    theirs = lax.dynamic_index_in_dim(halves, 1 - core, 1, False).reshape(half, -1)
    ours = lax.dynamic_index_in_dim(halves, core, 1, False).reshape(half, -1)
    away = jnp.dot(theirs, bases, preferred_element_type=F32)
    arrived = lax.ppermute(away, "core", [(0, 1), (1, 0)])
    kept = jnp.dot(ours, bases, preferred_element_type=F32)
    kept = lax.optimization_barrier(kept)
    blocks = (kept + arrived).reshape(X, half // X, -1)
    my_tokens = sum_blocks(exchange(blocks, "x")).astype(BF16)
    return lax.all_gather(my_tokens, TENSOR, axis=0, tiled=True)


def basis_of_all_y(bases):
    rows = bases.shape[0] // 8
    z = lax.axis_index("zh") * ZL + lax.axis_index("zl")
    piece = lax.dynamic_slice_in_dim(bases, (z % 8) * rows, rows, 0)
    core, x = lax.axis_index("core"), lax.axis_index("x")
    other = lax.ppermute(piece, "core", [(0, 1), (1, 0)])
    block = jnp.where(core == z // 8, piece, other)
    blocks = [block] + [lax.ppermute(block, "x", [(i, (i + d) % X) for i in range(X)]) for d in range(1, X)]
    blocks = jnp.stack(blocks)
    blocks = jnp.concatenate([lax.dynamic_index_in_dim(blocks, (x - k) % X, 0) for k in range(X)])
    return blocks.reshape(X * rows, -1)


def per_device(features, out_grads, bases, moment_one, moment_two):
    basis_rows = basis_of_all_y(bases)
    projected_low = project(features, bases)
    partial_sum = lax.dot_general(
        projected_low, out_grads, (((0,), (0,)), ((), ())), preferred_element_type=F32
    ).astype(BF16)
    rank, columns = partial_sum.shape
    own = rank // (Y * ZH * ZL)
    blocks = partial_sum.reshape(Y, ZH, ZL, own, columns).transpose(0, 2, 1, 3, 4)
    blocks = blocks.reshape(Y * ZL, ZH * own, columns)
    near = sum_blocks(exchange(blocks, ("y", "zl"))).astype(BF16)
    reduced = sum_blocks(exchange(near.reshape(ZH, own, columns), "zh"))
    new_moment_one = 0.9 * moment_one + 0.1 * reduced
    new_moment_two = 0.999 * moment_two + 0.001 * reduced * reduced
    first_fix = 1.0 - 0.9**STEP
    second_fix = 1.0 - 0.999**STEP
    direction = (
        new_moment_one / first_fix / (jnp.sqrt(new_moment_two / second_fix) + 1e-08)
    ).astype(BF16)
    quarter = columns // Y
    quarters = direction.reshape(own, Y, quarter).transpose(1, 0, 2)
    copies = jnp.broadcast_to(quarters[:, None], (Y, ZH * ZL, own, quarter))
    copies = copies.reshape(Y * ZH * ZL, own, quarter)
    my_quarter = exchange(copies, DP).reshape(rank, quarter)
    tile = jnp.dot(basis_rows, my_quarter, preferred_element_type=F32).astype(BF16)
    tiles = exchange(tile.reshape(Y, -1, quarter), "y")
    update = tiles.transpose(1, 0, 2).reshape(-1, columns)
    return (update, new_moment_one, new_moment_two)


def solution(mesh):
    split = Mesh(mesh.devices.reshape(Y, ZH, ZL, X, C), AXES)
    cut = P(DP, TENSOR)
    return jax.shard_map(
        per_device,
        mesh=split,
        in_specs=(cut, cut, P(TENSOR, None), cut, cut),
        out_specs=(cut, cut, cut),
        check_vma=False,
    )
```

```python
import jax
import jax.numpy as jnp
from jax import lax
from jax.sharding import Mesh, PartitionSpec as P

STEP = 100
Y, ZH, ZL, X, C = 4, 8, 2, 4, 2
BF16 = jnp.bfloat16
F32 = jnp.float32
AXES = ("y", "zh", "zl", "x", "core")
DP = ("y", "zh", "zl")
TENSOR = ("x", "core")


def exchange(blocks, axes):
    return lax.all_to_all(blocks, axes, 0, 0)


def sum_blocks(blocks):
    return jnp.sum(blocks.astype(F32), axis=0)


def project(features, bases):
    half = features.shape[0] // C
    core = lax.axis_index("core")
    halves = features.reshape(X, C, half // X, -1)
    theirs = lax.dynamic_index_in_dim(halves, 1 - core, 1, False).reshape(half, -1)
    ours = lax.dynamic_index_in_dim(halves, core, 1, False).reshape(half, -1)
    away = jnp.dot(theirs, bases, preferred_element_type=F32)
    arrived = lax.ppermute(away, "core", [(0, 1), (1, 0)])
    kept = jnp.dot(ours, bases, preferred_element_type=F32)
    kept = lax.optimization_barrier(kept)
    blocks = (kept + arrived).reshape(X, half // X, -1)
    my_tokens = sum_blocks(exchange(blocks, "x")).astype(BF16)
    return lax.all_gather(my_tokens, TENSOR, axis=0, tiled=True)


def basis_rows_of_pair(bases):
    rows = bases.shape[0] // 8 * ZL
    zh = lax.axis_index("zh")
    x = lax.axis_index("x")
    piece = lax.dynamic_slice_in_dim(bases, (zh % 4) * rows, rows, 0)
    other = lax.ppermute(piece, "core", [(0, 1), (1, 0)])
    block = jnp.where(lax.axis_index("core") == zh // 4, piece, other)
    blocks = [block]
    for step in range(1, X):
        pairs = [(i, (i + step) % X) for i in range(X)]
        blocks.append(lax.ppermute(block, "x", pairs))
    stacked = jnp.stack(blocks)
    return jnp.concatenate(
        [lax.dynamic_index_in_dim(stacked, (x - i) % X, 0, False) for i in range(X)]
    )


def per_device(features, out_grads, bases, moment_one, moment_two):
    basis_rows = basis_rows_of_pair(bases)
    projected_low = project(features, bases)
    partial_sum = lax.dot_general(
        projected_low, out_grads, (((0,), (0,)), ((), ())), preferred_element_type=F32
    ).astype(BF16)
    rank, columns = partial_sum.shape
    own = rank // (Y * ZH * ZL)
    blocks = partial_sum.reshape(Y, ZH, ZL, own, columns).transpose(0, 2, 1, 3, 4)
    blocks = blocks.reshape(Y * ZL, ZH * own, columns)
    near = sum_blocks(exchange(blocks, ("y", "zl"))).astype(BF16)
    reduced = sum_blocks(exchange(near.reshape(ZH, own, columns), "zh"))
    new_moment_one = 0.9 * moment_one + 0.1 * reduced
    new_moment_two = 0.999 * moment_two + 0.001 * reduced * reduced
    first_fix = 1.0 - 0.9**STEP
    second_fix = 1.0 - 0.999**STEP
    direction = (
        new_moment_one / first_fix / (jnp.sqrt(new_moment_two / second_fix) + 1e-08)
    ).astype(BF16)
    parts = Y * ZL
    width = columns // parts
    pieces = direction.reshape(own, Y, 1, ZL, width).transpose(1, 2, 3, 0, 4)
    copies = jnp.broadcast_to(pieces, (Y, ZH, ZL, own, width))
    copies = copies.reshape(parts * ZH, own, width)
    my_columns = exchange(copies, DP).reshape(rank, width)
    tile = jnp.dot(basis_rows, my_columns, preferred_element_type=F32).astype(BF16)
    tiles = exchange(tile.reshape(parts, -1, width), ("y", "zl"))
    update = tiles.transpose(1, 0, 2).reshape(-1, columns)
    return (update, new_moment_one, new_moment_two)


def solution(mesh):
    split = Mesh(mesh.devices.reshape(Y, ZH, ZL, X, C), AXES)
    cut = P(DP, TENSOR)
    return jax.shard_map(
        per_device,
        mesh=split,
        in_specs=(cut, cut, P(TENSOR, None), cut, cut),
        out_specs=(cut, cut, cut),
        check_vma=False,
    )
```

```python
import jax
import jax.numpy as jnp
from jax import lax
from jax.experimental import pallas as pl
from jax.experimental.pallas import tpu as pltpu
from jax.sharding import Mesh, PartitionSpec as P

STEP = 100
Y, ZH, ZL, X, C = 4, 8, 2, 4, 2
BF16 = jnp.bfloat16
F32 = jnp.float32
AXES = ("y", "zh", "zl", "x", "core")
DP = ("y", "zh", "zl")
TENSOR = ("x", "core")


def exchange(blocks, axes):
    return lax.all_to_all(blocks, axes, 0, 0)


def sum_blocks(blocks):
    return jnp.sum(blocks.astype(F32), axis=0)


def project(features, bases):
    half = features.shape[0] // C
    first, own_core = pair_place(bases)
    features, first, own_core = lax.optimization_barrier((features, first, own_core))
    core = lax.axis_index("core")
    halves = features.reshape(X, C, half // X, -1)
    theirs = lax.dynamic_index_in_dim(halves, 1 - core, 1, False).reshape(half, -1)
    ours = lax.dynamic_index_in_dim(halves, core, 1, False).reshape(half, -1)
    away = jnp.dot(theirs, bases, preferred_element_type=F32)
    arrived = lax.ppermute(away, "core", [(0, 1), (1, 0)])
    kept = jnp.dot(ours, bases, preferred_element_type=F32)
    kept = lax.optimization_barrier(kept)
    blocks = (kept + arrived).reshape(X, half // X, -1)
    my_tokens = sum_blocks(exchange(blocks, "x")).astype(BF16)
    my_tokens, bases = lax.optimization_barrier((my_tokens, bases))
    block = basis_block_of_pair(bases, first, own_core)
    return lax.all_gather(my_tokens, TENSOR, axis=0, tiled=True), block


def pair_place(bases):
    zh = lax.axis_index("zh")
    return (zh % 4) * (bases.shape[0] // 8 * ZL), lax.axis_index("core") == zh // 4


def basis_block_of_pair(bases, first, own_core):
    rows = bases.shape[0] // 8 * ZL
    piece = lax.dynamic_slice_in_dim(
        bases, first, rows, 0, allow_negative_indices=False
    )
    other = lax.ppermute(piece, "core", [(0, 1), (1, 0)])
    return jnp.where(own_core, piece, other)


def from_all_x(block):
    x = lax.axis_index("x")
    blocks = [block]
    for step in range(1, X):
        pairs = [(i, (i + step) % X) for i in range(X)]
        blocks.append(lax.ppermute(block, "x", pairs))
    stacked = jnp.stack(blocks)
    return jnp.concatenate(
        [lax.dynamic_index_in_dim(stacked, (x - i) % X, 0, False) for i in range(X)]
    )


def adam_kernel(parts_ref, one_ref, two_ref, new_one_ref, new_two_ref, copies_ref):
    reduced = parts_ref[0].astype(F32)
    for place in range(1, ZH):
        reduced += parts_ref[place].astype(F32)
    new_one = 0.9 * one_ref[...] + 0.1 * reduced
    new_two = 0.999 * two_ref[...] + 0.001 * reduced * reduced
    new_one_ref[...] = new_one
    new_two_ref[...] = new_two
    first_fix = 1.0 - 0.9**STEP
    second_fix = 1.0 - 0.999**STEP
    direction = new_one / first_fix / (jnp.sqrt(new_two / second_fix) + 1e-08)
    width = copies_ref.shape[2]
    for part in range(Y * ZL):
        piece = direction[:, part * width : (part + 1) * width].astype(BF16)
        y, zl = part // ZL, part % ZL
        for zh in range(ZH):
            copies_ref[(y * ZH + zh) * ZL + zl] = piece


def per_device(features, out_grads, bases, moment_one, moment_two):
    projected_low, block = project(features, bases)
    partial_sum = lax.dot_general(
        projected_low, out_grads, (((0,), (0,)), ((), ())), preferred_element_type=F32
    ).astype(BF16)
    partial_sum, block = lax.optimization_barrier((partial_sum, block))
    basis_rows = from_all_x(block)
    rank, columns = partial_sum.shape
    own = rank // (Y * ZH * ZL)
    blocks = partial_sum.reshape(Y, ZH, ZL, own, columns).transpose(0, 2, 1, 3, 4)
    blocks = blocks.reshape(Y * ZL, ZH * own, columns)
    near = sum_blocks(exchange(blocks, ("y", "zl"))).astype(BF16)
    arrived = exchange(near.reshape(ZH, own, columns), "zh")
    parts = Y * ZL
    width = columns // parts
    vmem = pl.BlockSpec(memory_space=pltpu.VMEM)
    new_moment_one, new_moment_two, copies = pl.pallas_call(
        adam_kernel,
        in_specs=[vmem] * 3,
        out_specs=[vmem] * 3,
        out_shape=[
            jax.ShapeDtypeStruct((own, columns), F32),
            jax.ShapeDtypeStruct((own, columns), F32),
            jax.ShapeDtypeStruct((parts * ZH, own, width), BF16),
        ],
    )(arrived, moment_one, moment_two)
    my_columns = exchange(copies, DP).reshape(rank, width)
    tile = jnp.dot(basis_rows, my_columns, preferred_element_type=F32).astype(BF16)
    tiles = exchange(tile.reshape(parts, -1, width), ("y", "zl"))
    update = tiles.transpose(1, 0, 2).reshape(-1, columns)
    return (update, new_moment_one, new_moment_two)


def solution(mesh):
    split = Mesh(mesh.devices.reshape(Y, ZH, ZL, X, C), AXES)
    cut = P(DP, TENSOR)
    return jax.shard_map(
        per_device,
        mesh=split,
        in_specs=(cut, cut, P(TENSOR, None), cut, cut),
        out_specs=(cut, cut, cut),
        check_vma=False,
    )
```

```python
import jax
import jax.numpy as jnp
from jax import lax
from jax.experimental import pallas as pl
from jax.experimental.pallas import tpu as pltpu
from jax.sharding import Mesh, PartitionSpec as P

STEP = 100
Y, ZH, ZL, X, C = 4, 8, 2, 4, 2
BF16 = jnp.bfloat16
F32 = jnp.float32
AXES = ("y", "za", "zb", "zl", "x", "core")
DP = ("y", "za", "zb", "zl")
TENSOR = ("x", "core")


def exchange(blocks, axes):
    return lax.all_to_all(blocks, axes, 0, 0)


def sum_blocks(blocks):
    return jnp.sum(blocks.astype(F32), axis=0)


def project(features, bases):
    half = features.shape[0] // C
    first, own_core = pair_place(bases)
    features, first, own_core = lax.optimization_barrier((features, first, own_core))
    core = lax.axis_index("core")
    halves = features.reshape(X, C, half // X, -1)
    theirs = lax.dynamic_index_in_dim(halves, 1 - core, 1, False).reshape(half, -1)
    ours = lax.dynamic_index_in_dim(halves, core, 1, False).reshape(half, -1)
    away = jnp.dot(theirs, bases, preferred_element_type=F32)
    arrived = lax.ppermute(away, "core", [(0, 1), (1, 0)])
    kept = jnp.dot(ours, bases, preferred_element_type=F32)
    kept = lax.optimization_barrier(kept)
    blocks = (kept + arrived).reshape(X, half // X, -1)
    my_tokens = sum_blocks(exchange(blocks, "x")).astype(BF16)
    my_tokens, bases = lax.optimization_barrier((my_tokens, bases))
    block = basis_block_of_pair(bases, first, own_core)
    return lax.all_gather(my_tokens, TENSOR, axis=0, tiled=True), block


def pair_place(bases):
    zh = lax.axis_index(("za", "zb"))
    return (zh % 4) * (bases.shape[0] // 8 * ZL), lax.axis_index("core") == zh // 4


def basis_block_of_pair(bases, first, own_core):
    rows = bases.shape[0] // 8 * ZL
    piece = lax.dynamic_slice_in_dim(
        bases, first, rows, 0, allow_negative_indices=False
    )
    other = lax.ppermute(piece, "core", [(0, 1), (1, 0)])
    return jnp.where(own_core, piece, other)


def from_all_x(block):
    x = lax.axis_index("x")
    blocks = [block]
    for step in range(1, X):
        pairs = [(i, (i + step) % X) for i in range(X)]
        blocks.append(lax.ppermute(block, "x", pairs))
    stacked = jnp.stack(blocks)
    return jnp.concatenate(
        [lax.dynamic_index_in_dim(stacked, (x - i) % X, 0, False) for i in range(X)]
    )


def adam_kernel(parts_ref, one_ref, two_ref, new_one_ref, new_two_ref, copies_ref):
    reduced = parts_ref[0].astype(F32)
    for place in range(1, ZH):
        reduced += parts_ref[place].astype(F32)
    new_one = 0.9 * one_ref[...] + 0.1 * reduced
    new_two = 0.999 * two_ref[...] + 0.001 * reduced * reduced
    new_one_ref[...] = new_one
    new_two_ref[...] = new_two
    first_fix = 1.0 - 0.9**STEP
    second_fix = 1.0 - 0.999**STEP
    direction = new_one / first_fix / (jnp.sqrt(new_two / second_fix) + 1e-08)
    width = copies_ref.shape[2]
    for part in range(Y * ZL):
        piece = direction[:, part * width : (part + 1) * width].astype(BF16)
        y, zl = part // ZL, part % ZL
        for zh in range(ZH):
            copies_ref[(y * ZH + zh) * ZL + zl] = piece


def per_device(features, out_grads, bases, moment_one, moment_two):
    projected_low, block = project(features, bases)
    partial_sum = lax.dot_general(
        projected_low, out_grads, (((0,), (0,)), ((), ())), preferred_element_type=F32
    ).astype(BF16)
    partial_sum, block = lax.optimization_barrier((partial_sum, block))
    basis_rows = from_all_x(block)
    rank, columns = partial_sum.shape
    own = rank // (Y * ZH * ZL)
    blocks = partial_sum.reshape(Y, ZH // 2, 2, ZL, own, columns)
    blocks = blocks.transpose(0, 3, 2, 1, 4, 5)
    blocks = blocks.reshape(Y * ZL, ZH * own, columns)
    near = sum_blocks(exchange(blocks, ("y", "zl"))).astype(BF16)
    arrived = exchange(near.reshape(ZH, own, columns), ("zb", "za"))
    parts = Y * ZL
    width = columns // parts
    vmem = pl.BlockSpec(memory_space=pltpu.VMEM)
    new_moment_one, new_moment_two, copies = pl.pallas_call(
        adam_kernel,
        in_specs=[vmem] * 3,
        out_specs=[vmem] * 3,
        out_shape=[
            jax.ShapeDtypeStruct((own, columns), F32),
            jax.ShapeDtypeStruct((own, columns), F32),
            jax.ShapeDtypeStruct((parts * ZH, own, width), BF16),
        ],
    )(arrived, moment_one, moment_two)
    my_columns = exchange(copies, DP).reshape(rank, width)
    tile = jnp.dot(basis_rows, my_columns, preferred_element_type=F32).astype(BF16)
    tiles = exchange(tile.reshape(parts, -1, width), ("y", "zl"))
    update = tiles.transpose(1, 0, 2).reshape(-1, columns)
    return (update, new_moment_one, new_moment_two)


def solution(mesh):
    split = Mesh(mesh.devices.reshape(Y, ZH // 2, 2, ZL, X, C), AXES)
    cut = P(DP, TENSOR)
    return jax.shard_map(
        per_device,
        mesh=split,
        in_specs=(cut, cut, P(TENSOR, None), cut, cut),
        out_specs=(cut, cut, cut),
        check_vma=False,
    )
```

```python
import jax
import jax.numpy as jnp
from jax import lax
from jax.experimental import pallas as pl
from jax.experimental.pallas import tpu as pltpu
from jax.sharding import Mesh, PartitionSpec as P

STEP = 100
Y, ZH, ZL, X, C = 4, 8, 2, 4, 2
BF16 = jnp.bfloat16
F32 = jnp.float32
AXES = ("y", "zh", "zl", "x", "core")
DP = ("y", "zh", "zl")
TENSOR = ("x", "core")


def exchange(blocks, axes):
    return lax.all_to_all(blocks, axes, 0, 0)


def sum_blocks(blocks):
    return jnp.sum(blocks.astype(F32), axis=0)


def project(features, bases):
    half = features.shape[0] // C
    first, own_core = pair_place(bases)
    features, first, own_core = lax.optimization_barrier((features, first, own_core))
    core = lax.axis_index("core")
    halves = features.reshape(X, C, half // X, -1)
    theirs = lax.dynamic_index_in_dim(halves, 1 - core, 1, False).reshape(half, -1)
    ours = lax.dynamic_index_in_dim(halves, core, 1, False).reshape(half, -1)
    away = jnp.dot(theirs, bases, preferred_element_type=F32)
    arrived = lax.ppermute(away, "core", [(0, 1), (1, 0)])
    kept = jnp.dot(ours, bases, preferred_element_type=F32)
    kept = lax.optimization_barrier(kept)
    blocks = (kept + arrived).reshape(X, half // X, -1)
    my_tokens = sum_blocks(exchange(blocks, "x")).astype(BF16)
    my_tokens, bases = lax.optimization_barrier((my_tokens, bases))
    pieces = basis_pieces_of_pair(bases, first) + (own_core,)
    return lax.all_gather(my_tokens, TENSOR, axis=0, tiled=True), pieces


def pair_place(bases):
    zh = lax.axis_index("zh")
    return (zh % 4) * (bases.shape[0] // 8 * ZL), lax.axis_index("core") == zh // 4


def basis_pieces_of_pair(bases, first):
    rows = bases.shape[0] // 8 * ZL
    piece = lax.dynamic_slice_in_dim(
        bases, first, rows, 0, allow_negative_indices=False
    )
    return piece, lax.ppermute(piece, "core", [(0, 1), (1, 0)])


def from_all_x(block):
    x = lax.axis_index("x")
    blocks = [block]
    for step in range(1, X):
        pairs = [(i, (i + step) % X) for i in range(X)]
        blocks.append(lax.ppermute(block, "x", pairs))
    stacked = jnp.stack(blocks)
    return jnp.concatenate(
        [lax.dynamic_index_in_dim(stacked, (x - i) % X, 0, False) for i in range(X)]
    )


def adam_kernel(parts_ref, one_ref, two_ref, new_one_ref, new_two_ref, copies_ref):
    reduced = parts_ref[0].astype(F32)
    for place in range(1, ZH):
        reduced += parts_ref[place].astype(F32)
    new_one = 0.9 * one_ref[...] + 0.1 * reduced
    new_two = 0.999 * two_ref[...] + 0.001 * reduced * reduced
    new_one_ref[...] = new_one
    new_two_ref[...] = new_two
    first_fix = 1.0 - 0.9**STEP
    second_fix = 1.0 - 0.999**STEP
    direction = new_one / first_fix / (jnp.sqrt(new_two / second_fix) + 1e-08)
    width = copies_ref.shape[2]
    for part in range(Y * ZL):
        piece = direction[:, part * width : (part + 1) * width].astype(BF16)
        y, zl = part // ZL, part % ZL
        for zh in range(ZH):
            copies_ref[(y * ZH + zh) * ZL + zl] = piece


def per_device(features, out_grads, bases, moment_one, moment_two):
    projected_low, pieces = project(features, bases)
    partial_sum = lax.dot_general(
        projected_low, out_grads, (((0,), (0,)), ((), ())), preferred_element_type=F32
    ).astype(BF16)
    partial_sum, pieces = lax.optimization_barrier((partial_sum, pieces))
    piece, other, own_core = pieces
    basis_rows = from_all_x(jnp.where(own_core, piece, other))
    rank, columns = partial_sum.shape
    own = rank // (Y * ZH * ZL)
    blocks = partial_sum.reshape(Y, ZH, ZL, own, columns).transpose(0, 2, 1, 3, 4)
    blocks = blocks.reshape(Y * ZL, ZH * own, columns)
    near = sum_blocks(exchange(blocks, ("y", "zl"))).astype(BF16)
    arrived = exchange(near.reshape(ZH, own, columns), "zh")
    parts = Y * ZL
    width = columns // parts
    vmem = pl.BlockSpec(memory_space=pltpu.VMEM)
    new_moment_one, new_moment_two, copies = pl.pallas_call(
        adam_kernel,
        in_specs=[vmem] * 3,
        out_specs=[vmem] * 3,
        out_shape=[
            jax.ShapeDtypeStruct((own, columns), F32),
            jax.ShapeDtypeStruct((own, columns), F32),
            jax.ShapeDtypeStruct((parts * ZH, own, width), BF16),
        ],
    )(arrived, moment_one, moment_two)
    my_columns = exchange(copies, DP).reshape(rank, width)
    tile = jnp.dot(basis_rows, my_columns, preferred_element_type=F32).astype(BF16)
    tiles = exchange(tile.reshape(parts, -1, width), ("y", "zl"))
    update = tiles.transpose(1, 0, 2).reshape(-1, columns)
    return (update, new_moment_one, new_moment_two)


def solution(mesh):
    split = Mesh(mesh.devices.reshape(Y, ZH, ZL, X, C), AXES)
    cut = P(DP, TENSOR)
    return jax.shard_map(
        per_device,
        mesh=split,
        in_specs=(cut, cut, P(TENSOR, None), cut, cut),
        out_specs=(cut, cut, cut),
        check_vma=False,
    )
```

```python
import jax
import jax.numpy as jnp
from jax import lax
from jax.experimental import pallas as pl
from jax.experimental.pallas import tpu as pltpu
from jax.sharding import Mesh, PartitionSpec as P

STEP = 100
Y, ZH, ZL, X, C = 4, 8, 2, 4, 2
BF16 = jnp.bfloat16
F32 = jnp.float32
AXES = ("y", "zh", "zl", "x", "core")
DP = ("y", "zh", "zl")
TENSOR = ("x", "core")


def exchange(blocks, axes):
    return lax.all_to_all(blocks, axes, 0, 0)


def sum_blocks(blocks):
    return jnp.sum(blocks.astype(F32), axis=0)


def project(features, bases):
    half = features.shape[0] // C
    first, own_core = pair_place(bases)
    features, first, own_core = lax.optimization_barrier((features, first, own_core))
    core = lax.axis_index("core")
    halves = features.reshape(X, C, half // X, -1)
    theirs = lax.dynamic_index_in_dim(halves, 1 - core, 1, False).reshape(half, -1)
    ours = lax.dynamic_index_in_dim(halves, core, 1, False).reshape(half, -1)
    away = jnp.dot(theirs, bases, preferred_element_type=F32)
    arrived = lax.ppermute(away, "core", [(0, 1), (1, 0)])
    kept = jnp.dot(ours, bases, preferred_element_type=F32)
    kept = lax.optimization_barrier(kept)
    blocks = (kept + arrived).reshape(X, half // X, -1)
    my_tokens = sum_blocks(exchange(blocks, "x")).astype(BF16)
    my_tokens, bases = lax.optimization_barrier((my_tokens, bases))
    block = basis_block_of_pair(bases, first, own_core)
    return lax.all_gather(my_tokens, TENSOR, axis=0, tiled=True), block


def pair_place(bases):
    zh = lax.axis_index("zh")
    return (zh % 4) * (bases.shape[0] // 8 * ZL), lax.axis_index("core") == zh // 4


def basis_block_of_pair(bases, first, own_core):
    rows = bases.shape[0] // 8 * ZL
    piece = lax.dynamic_slice_in_dim(
        bases, first, rows, 0, allow_negative_indices=False
    )
    other = lax.ppermute(piece, "core", [(0, 1), (1, 0)])
    return jnp.where(own_core, piece, other)


def from_all_x(block):
    x = lax.axis_index("x")
    blocks = [block]
    for step in range(1, X):
        pairs = [(i, (i + step) % X) for i in range(X)]
        blocks.append(lax.ppermute(block, "x", pairs))
    stacked = jnp.stack(blocks)
    return jnp.concatenate(
        [lax.dynamic_index_in_dim(stacked, (x - i) % X, 0, False) for i in range(X)]
    )


def adam_kernel(parts_ref, one_ref, two_ref, new_one_ref, new_two_ref, copies_ref):
    reduced = parts_ref[0].astype(F32)
    for place in range(1, ZH):
        reduced += parts_ref[place].astype(F32)
    new_one = 0.9 * one_ref[...] + 0.1 * reduced
    new_two = 0.999 * two_ref[...] + 0.001 * reduced * reduced
    new_one_ref[...] = new_one
    new_two_ref[...] = new_two
    first_fix = 1.0 - 0.9**STEP
    second_fix = 1.0 - 0.999**STEP
    direction = new_one / first_fix / (jnp.sqrt(new_two / second_fix) + 1e-08)
    width = copies_ref.shape[2]
    for part in range(Y * ZL):
        piece = direction[:, part * width : (part + 1) * width].astype(BF16)
        y, zl = part // ZL, part % ZL
        for zh in range(ZH):
            copies_ref[(y * ZH + zh) * ZL + zl] = piece


def per_device(features, out_grads, bases, moment_one, moment_two):
    projected_low, block = project(features, bases)
    partial_sum = lax.dot_general(
        projected_low, out_grads, (((0,), (0,)), ((), ())), preferred_element_type=F32
    ).astype(BF16)
    partial_sum, block = lax.optimization_barrier((partial_sum, block))
    basis_rows = from_all_x(block)
    rank, columns = partial_sum.shape
    own = rank // (Y * ZH * ZL)
    blocks = partial_sum.reshape(Y, ZH, ZL, own, columns).transpose(0, 2, 1, 3, 4)
    lanes = 128
    blocks = blocks.reshape(Y * ZL, ZH, own, columns // lanes, lanes)
    blocks = blocks.transpose(0, 1, 3, 2, 4).reshape(Y * ZL, -1, lanes)
    near = sum_blocks(exchange(blocks, ("y", "zl"))).astype(BF16)
    near = near.reshape(ZH, columns // lanes, own, lanes).transpose(0, 2, 1, 3)
    arrived = exchange(near.reshape(ZH, own, columns), "zh")
    parts = Y * ZL
    width = columns // parts
    vmem = pl.BlockSpec(memory_space=pltpu.VMEM)
    new_moment_one, new_moment_two, copies = pl.pallas_call(
        adam_kernel,
        in_specs=[vmem] * 3,
        out_specs=[vmem] * 3,
        out_shape=[
            jax.ShapeDtypeStruct((own, columns), F32),
            jax.ShapeDtypeStruct((own, columns), F32),
            jax.ShapeDtypeStruct((parts * ZH, own, width), BF16),
        ],
    )(arrived, moment_one, moment_two)
    my_columns = exchange(copies, DP).reshape(rank, width)
    tile = jnp.dot(basis_rows, my_columns, preferred_element_type=F32).astype(BF16)
    tiles = exchange(tile.reshape(parts, -1, width), ("y", "zl"))
    update = tiles.transpose(1, 0, 2).reshape(-1, columns)
    return (update, new_moment_one, new_moment_two)


def solution(mesh):
    split = Mesh(mesh.devices.reshape(Y, ZH, ZL, X, C), AXES)
    cut = P(DP, TENSOR)
    return jax.shard_map(
        per_device,
        mesh=split,
        in_specs=(cut, cut, P(TENSOR, None), cut, cut),
        out_specs=(cut, cut, cut),
        check_vma=False,
    )
```
